256 devices in a mesh: row: 64 (over z, x, core), col: 4 (over y).
Axes of the slice: x: 4, y: 4, z: 8, core: 2. Of those that a mesh axis runs over, the one named last changes fastest.
Arguments:
- diagonal: float32 [256, 512, 512], P(('row', 'col')), may hold values from -0.05 to 1.05
- lower: float32 [256, 512, 512], P(('row', 'col')), may hold values from -1 to 1, as said below
- upper: float32 [256, 512, 512], P(('row', 'col')), may hold values from -1 to 1, as said below
- right_side: float32 [256, 512, 128], P(('row', 'col')), may hold values from -6 to 6
- guess: float32 [256, 512, 128], P(('row', 'col')), may hold values from -4 to 4
Outputs:
- solution: float32 [256, 512, 128], P(('row', 'col'))
The draws below stay inside these ranges and needn't reach their ends.
Inputs may be any that keep to these rules, and one draw needn't show every extreme that they name: `lower`: each block is one half of an orthogonal matrix. `upper`: each block is one half of an orthogonal matrix.
All inputs are finite; a program needn't handle non-finite values.
Results may differ from the reference program's by a relative error of at most 0.00026.
Values sent between devices are 32-bit elements; how exact they have to be, the bound alone decides.
No kernel may reach another device: no remote copies, remote signals or barrier semaphores. Data moves between devices by JAX's collectives and lax.ppermute only.
A program may use at most 64 MiB of HBM per device.

```python
import jax
import jax.numpy as jnp
from jax import lax

B = 512
R = 128
LEVELS = 2
NEWTON = 2
NB = 256


def draw_diagonal(key, part):
    scale = 0.025 / B ** 0.5
    shift_key = jax.random.fold_in(key, 5)
    noise_key = jax.random.fold_in(key, 7)
    shift = jax.random.uniform(shift_key, (NB,), jnp.float32, 1.004, 1.009)
    noise = jnp.clip(jax.random.normal(noise_key, (NB, B, B), jnp.float32), -6.0, 6.0) * scale
    return shift[:, None, None] * jnp.eye(B, dtype=jnp.float32) + noise


def half_orthogonal(key):
    gauss = jax.random.normal(key, (NB, B, B), jnp.float32)
    basis, upper_tri = jnp.linalg.qr(gauss)
    signs = jnp.sign(jnp.diagonal(upper_tri, axis1=1, axis2=2)) + (jnp.diagonal(upper_tri, axis1=1, axis2=2) == 0)
    return 0.5 * basis * signs[:, None, :]


def coupling_basis(key):
    return half_orthogonal(jax.random.fold_in(key, 11))


def draw_lower(key, part):
    return -coupling_basis(key)


def draw_upper(key, part):
    following = jnp.roll(coupling_basis(key), -1, axis=0)
    return -jnp.swapaxes(following, 1, 2)


def level_of(key, shape, shards, smallest, largest):
    def one(dim, blocks):
        heights = jax.random.uniform(jax.random.fold_in(jax.random.fold_in(key, 6), dim), (blocks,), jnp.float32, smallest / len(shards), largest / len(shards))
        return jnp.repeat(jnp.exp(heights), shape[dim] // blocks).reshape((-1,) + (1,) * (len(shape) - dim - 1))

    factor_of = one(*shards[0])
    for cut in shards[1:]:
        factor_of = factor_of * one(*cut)
    return factor_of


def scatter_about(stream_key, extent, deviation, most, cuts=(), held_as=jnp.bfloat16):
    drawn = jax.random.normal(stream_key, extent, jnp.float32) * deviation
    if len(cuts) > 0:
        drawn = level_of(stream_key, extent, cuts, -0.22, 0.18) * drawn
    return jnp.clip(drawn, min=-most, max=most).astype(held_as)


def setup_inputs(seed: int = 0) -> dict:
    streams_of = jax.random.split(jax.random.key(seed), 6)
    return {
        "diagonal": draw_diagonal(jax.random.fold_in(streams_of[5], 71), 0),
        "lower": draw_lower(jax.random.fold_in(streams_of[5], 71), 0),
        "upper": draw_upper(jax.random.fold_in(streams_of[5], 71), 0),
        "right_side": scatter_about(streams_of[3], (NB, B, R), 1.0, 6.0, ((0, 256),), jnp.float32),
        "guess": scatter_about(streams_of[4], (NB, B, R), 1.0, 4.0, ((0, 256),), jnp.float32),
    }


def multiply(left, right):
    return jnp.matmul(left, right, precision=lax.Precision.HIGHEST)

def invert(matrix):
    order = matrix.shape[-1]
    eye = jnp.eye(order, dtype=jnp.float32)
    mean_diag = jnp.trace(matrix, axis1=-2, axis2=-1) / order
    approx = eye / mean_diag[..., None, None]
    for step in range(NEWTON):
        approx = multiply(approx, 2.0 * eye - multiply(matrix, approx))
    return approx

def from_before(array, stride):
    return jnp.concatenate([jnp.zeros_like(array[:stride]), array[:-stride]], axis=0)

def from_after(array, stride):
    return jnp.concatenate([array[stride:], jnp.zeros_like(array[:stride])], axis=0)

def reference(diagonal, lower, upper, right_side, guess):
    count = diagonal.shape[0]
    rows = jnp.arange(count, dtype=jnp.int32)[:, None, None]
    low = jnp.where(rows == 0, jnp.float32(0.0), lower)
    up = jnp.where(rows == count - 1, jnp.float32(0.0), upper)
    diag = diagonal
    rhs = right_side
    for level in range(LEVELS):
        stride = 2 ** level
        pivot = invert(diag)
        scaled_low = multiply(pivot, low)
        scaled_up = multiply(pivot, up)
        scaled_rhs = multiply(pivot, rhs)
        new_diag = diag - multiply(low, from_before(scaled_up, stride)) - multiply(up, from_after(scaled_low, stride))
        new_rhs = rhs - multiply(low, from_before(scaled_rhs, stride)) - multiply(up, from_after(scaled_rhs, stride))
        new_low = -multiply(low, from_before(scaled_low, stride))
        new_up = -multiply(up, from_after(scaled_up, stride))
        diag, low, up, rhs = (new_diag, new_low, new_up, new_rhs)
    reach = 2 ** LEVELS
    inner = rhs - multiply(low, from_before(guess, reach)) - multiply(up, from_after(guess, reach))
    return multiply(invert(diag), inner)
```

```python
import jax
import jax.numpy as jnp
from jax import lax
from jax.sharding import PartitionSpec as P

AXES = ("row", "col")


def shifted(value, steps):
    count = lax.axis_size(AXES)
    initial, last = (max(0, -steps), min(count, count - steps))
    return lax.ppermute(value, AXES, [(source, source + steps) for source in range(initial, last)])


def multiply(left, right):
    return jnp.dot(left, right, precision=lax.Precision.HIGH, preferred_element_type=jnp.float32)


def residual(matrix):
    order = matrix.shape[-1]
    scale = order / jnp.trace(matrix)
    return jnp.eye(order, dtype=jnp.float32) - matrix * scale, scale


def invert(matrix):
    rest, scale = residual(matrix)
    square = multiply(rest, rest)
    eye = jnp.eye(matrix.shape[-1], dtype=jnp.float32)
    return (eye + rest + square + multiply(rest, square)) * scale


def body(diagonal, lower, upper, right_side, guess):
    chain = lax.axis_size(AXES)
    place = lax.axis_index(AXES)
    diag = diagonal[0]
    low = jnp.where(place == 0, jnp.float32(0.0), lower[0])
    up = jnp.where(place == chain - 1, jnp.float32(0.0), upper[0])
    rhs = right_side[0]
    cols = rhs.shape[1]
    guess_l = shifted(guess[0], 1)
    guess_r = shifted(guess[0], -1)
    pivot = invert(diag)
    scaled_up = multiply(pivot, up)
    scaled_low = multiply(pivot, low)
    up_l = shifted(scaled_up, 1)
    low_r = shifted(scaled_low, -1)
    scaled_rhs = multiply(pivot, rhs)
    vec_l = shifted(jnp.concatenate([scaled_rhs, multiply(scaled_low, guess_l)], axis=1), 1)
    vec_r = shifted(jnp.concatenate([scaled_rhs, multiply(scaled_up, guess_r)], axis=1), -1)
    diag1 = diag - multiply(low, up_l) - multiply(up, low_r)
    pivot1 = invert(diag1)
    next_l = shifted(multiply(pivot1, up), 1)
    next_r = shifted(multiply(pivot1, low), -1)
    lv = multiply(low, vec_l)
    uv = multiply(up, vec_r)
    rhs1 = rhs - lv[:, :cols] - uv[:, :cols]
    w_l = shifted(multiply(pivot1, rhs1 + lv[:, cols:]), 1)
    w_r = shifted(multiply(pivot1, rhs1 + uv[:, cols:]), -1)
    pass_l = shifted(multiply(scaled_low, next_l), 1)
    pass_r = shifted(multiply(scaled_up, next_r), -1)
    d_l = shifted(multiply(scaled_low, w_l), 1)
    d_r = shifted(multiply(scaled_up, w_r), -1)
    diag2 = diag1 - multiply(multiply(low, pass_l), up_l) - multiply(multiply(up, pass_r), low_r)
    inner = rhs1 + multiply(low, d_l) + multiply(up, d_r)
    rest, scale = residual(diag2)
    part = inner + multiply(rest, multiply(rest, inner))
    return ((part + multiply(rest, part)) * scale)[None]


def solution(mesh):
    spec = P(AXES, None, None)
    return jax.shard_map(
        body,
        mesh=mesh,
        in_specs=(spec,) * 5,
        out_specs=spec,
        check_vma=False,
    )
```

```python
import jax
import jax.numpy as jnp
from jax import lax
from jax.experimental import pallas as pl
from jax.experimental.pallas import tpu as pltpu
from jax.sharding import PartitionSpec as P

AXES = ("row", "col")

VECTOR_WEIGHT = 10**10
PASS_WEIGHT = 10**10
MIDDLE_WEIGHT = 10**10

VMEM_LIMIT = 24 * 1024 * 1024
FIRST_LIMIT = 60 * 1024 * 1024


def shifted(value, steps):
    count = lax.axis_size(AXES)
    initial, last = (max(0, -steps), min(count, count - steps))
    return lax.ppermute(value, AXES, [(source, source + steps) for source in range(initial, last)])


def split(value):
    high = value.astype(jnp.bfloat16)
    return high, (value - high.astype(jnp.float32)).astype(jnp.bfloat16)


def multiply(left, right):
    (lh, ll), (rh, rl) = left, right
    cols = rh.shape[1]
    if cols <= 128:
        both = dot(lh, jnp.concatenate([rh, rl], axis=1))
        return both[:, :cols] + (both[:, cols:] + dot(ll, rh))
    return dot(lh, rh) + (dot(lh, rl) + dot(ll, rh))


def dot(left, right):
    return jnp.dot(left, right, preferred_element_type=jnp.float32)


def on_diagonal(order):
    rows = lax.broadcasted_iota(jnp.int32, (order, order), 0)
    return rows == lax.broadcasted_iota(jnp.int32, (order, order), 1)


def residual(matrix):
    order = matrix.shape[-1]
    same = on_diagonal(order)
    picked = jnp.where(same, matrix, 0.0)
    total = jnp.sum(jnp.sum(picked, axis=0, keepdims=True), axis=1, keepdims=True)
    scale = order / total
    return jnp.where(same, 1.0, 0.0) - matrix * scale, scale


def invert(matrix):
    rest, scale = residual(matrix)
    halves = split(rest)
    square = multiply(halves, halves)
    cube = multiply(halves, split(square))
    eye = jnp.where(on_diagonal(matrix.shape[-1]), 1.0, 0.0)
    return (eye + (rest + (square + cube))) * scale


def first_kernel(diag, low, up, rhs, scaled_up, scaled_low, scaled_rhs, diag_v, low_v, up_v, rhs_v, sems):
    pairs = ((diag, diag_v), (up, up_v), (low, low_v), (rhs, rhs_v))
    copies = [pltpu.make_async_copy(*pair, sems.at[place]) for place, pair in enumerate(pairs)]
    for copy in copies:
        copy.start()
    copies[0].wait()
    pivot = split(invert(diag_v[...]))
    copies[1].wait()
    scaled_up[...] = multiply(pivot, split(up_v[...]))
    copies[2].wait()
    scaled_low[...] = multiply(pivot, split(low_v[...]))
    copies[3].wait()
    scaled_rhs[...] = multiply(pivot, split(rhs_v[...]))


def vector_kernel(scaled_up, scaled_low, scaled_rhs, guess_l, guess_r, to_up, to_down):
    cols = scaled_rhs.shape[1]
    value = scaled_rhs[...]
    to_up[:, :cols] = value
    to_down[:, :cols] = value
    to_up[:, cols:] = multiply(split(scaled_low[...]), split(guess_l[...]))
    to_down[:, cols:] = multiply(split(scaled_up[...]), split(guess_r[...]))


def second_kernel(diag, low, up, up_l, low_r, diag1, pivot1, to_up, to_down):
    low_halves, up_halves = split(low[...]), split(up[...])
    value = diag[...] - multiply(low_halves, split(up_l[...])) - multiply(up_halves, split(low_r[...]))
    diag1[...] = value
    pivot = invert(value)
    pivot1[...] = pivot
    halves = split(pivot)
    to_up[...] = multiply(halves, up_halves)
    to_down[...] = multiply(halves, low_halves)


def middle_kernel(low, up, rhs, pivot1, vec_l, vec_r, rhs1, to_up, to_down):
    cols = rhs.shape[1]
    lv = multiply(split(low[...]), split(vec_l[...]))
    uv = multiply(split(up[...]), split(vec_r[...]))
    value = rhs[...] - lv[:, :cols] - uv[:, :cols]
    rhs1[...] = value
    pivot = split(pivot1[...])
    to_up[...] = multiply(pivot, split(value + lv[:, cols:]))
    to_down[...] = multiply(pivot, split(value + uv[:, cols:]))


def pair_kernel(left, right, out):
    out[...] = multiply(split(left[...]), split(right[...]))


def two_pairs_kernel(left_a, right_a, left_b, right_b, out_a, out_b):
    out_a[...] = multiply(split(left_a[...]), split(right_a[...]))
    out_b[...] = multiply(split(left_b[...]), split(right_b[...]))


def inner_kernel(rhs1, low, up, d_l, d_r, out):
    out[...] = rhs1[...] + multiply(split(low[...]), split(d_l[...])) + multiply(split(up[...]), split(d_r[...]))


def triple(first, second, third):
    return multiply(split(multiply(split(first), split(second))), split(third))


def before_last_kernel(base, first, second, third, out):
    out[...] = base[...] - triple(first[...], second[...], third[...])


def last_kernel(base, first, second, third, inner_ref, out):
    rest, scale = residual(base[...] - triple(first[...], second[...], third[...]))
    halves = split(rest)
    inner = inner_ref[...]
    part = inner + multiply(halves, split(multiply(halves, split(inner))))
    out[...] = (part + multiply(halves, split(part))) * scale


def call(kernel, outs, *args, weight=0, limit=VMEM_LIMIT, **options):
    in_vmem = pl.BlockSpec(memory_space=pltpu.VMEM)
    options = {"in_specs": [in_vmem] * len(args)} | options
    return pl.pallas_call(
        kernel,
        out_shape=[jax.ShapeDtypeStruct(shape, jnp.float32) for shape in outs],
        out_specs=[in_vmem] * len(outs),
        compiler_params=pltpu.CompilerParams(vmem_limit_bytes=limit),
        cost_estimate=pl.CostEstimate(flops=weight, bytes_accessed=0, transcendentals=0),
        **options,
    )(*args)


def body(diagonal, lower, upper, right_side, guess):
    diag, low, up, rhs = diagonal[0], lower[0], upper[0], right_side[0]
    square, tall = diag.shape, rhs.shape
    wide = (tall[0], 2 * tall[1])
    guess_l = shifted(guess[0], 1)
    guess_r = shifted(guess[0], -1)
    scaled_up, scaled_low, scaled_rhs = call(
        first_kernel,
        (square, square, tall),
        *(diag, low, up, rhs),
        limit=FIRST_LIMIT,
        in_specs=[pl.BlockSpec(memory_space=pl.ANY)] * 4,
        scratch_shapes=[pltpu.VMEM(shape, jnp.float32) for shape in (square, square, square, tall)]
        + [pltpu.SemaphoreType.DMA((4,))],
    )
    up_l = shifted(scaled_up, 1)
    low_r = shifted(scaled_low, -1)
    to_up, to_down = call(
        vector_kernel, (wide, wide), scaled_up, scaled_low, scaled_rhs, guess_l, guess_r, weight=VECTOR_WEIGHT
    )
    vec_l = shifted(to_up, 1)
    vec_r = shifted(to_down, -1)
    diag1, pivot1, next_up, next_down = call(second_kernel, (square,) * 4, diag, low, up, up_l, low_r)
    next_l = shifted(next_up, 1)
    next_r = shifted(next_down, -1)
    rhs1, w_up, w_down = call(
        middle_kernel, (tall,) * 3, low, up, rhs, pivot1, vec_l, vec_r, weight=MIDDLE_WEIGHT
    )
    w_l = shifted(w_up, 1)
    w_r = shifted(w_down, -1)
    scaled_low, scaled_up, _, _ = lax.optimization_barrier((scaled_low, scaled_up, w_up, w_down))
    (pass_up,) = call(pair_kernel, (square,), scaled_low, next_l)
    (pass_down,) = call(pair_kernel, (square,), scaled_up, next_r)
    pass_l = shifted(pass_up, 1)
    pass_r = shifted(pass_down, -1)
    w_l, w_r, _, _ = lax.optimization_barrier((w_l, w_r, pass_up, pass_down))
    d_up, d_down = call(two_pairs_kernel, (tall, tall), scaled_low, w_l, scaled_up, w_r, weight=PASS_WEIGHT)
    d_l = shifted(d_up, 1)
    d_r = shifted(d_down, -1)
    (inner,) = call(inner_kernel, (tall,), rhs1, low, up, d_l, d_r)
    (part2,) = call(before_last_kernel, (square,), diag1, low, pass_l, up_l)
    part2, inner = lax.optimization_barrier((part2, inner))
    (out,) = call(last_kernel, (tall,), part2, up, pass_r, low_r, inner)
    return out[None]


def solution(mesh):
    spec = P(AXES, None, None)
    return jax.shard_map(
        body,
        mesh=mesh,
        in_specs=(spec,) * 5,
        out_specs=spec,
        check_vma=False,
    )
```

```python
import jax
import jax.numpy as jnp
from jax import lax
from jax.experimental import pallas as pl
from jax.experimental.pallas import tpu as pltpu
from jax.sharding import PartitionSpec as P

AXES = ("row", "col")

VECTOR_WEIGHT = 10**10
PASS_WEIGHT = 10**10
MIDDLE_WEIGHT = 10**10

VMEM_LIMIT = 24 * 1024 * 1024
FIRST_LIMIT = 60 * 1024 * 1024


def shifted(value, steps):
    count = lax.axis_size(AXES)
    initial, last = (max(0, -steps), min(count, count - steps))
    return lax.ppermute(value, AXES, [(source, source + steps) for source in range(initial, last)])


def split(value):
    high = value.astype(jnp.bfloat16)
    return high, (value - high.astype(jnp.float32)).astype(jnp.bfloat16)


def multiply(left, right):
    (lh, ll), (rh, rl) = left, right
    cols = rh.shape[1]
    if cols <= 128:
        both = dot(lh, jnp.concatenate([rh, rl], axis=1))
        return both[:, :cols] + (both[:, cols:] + dot(ll, rh))
    return dot(lh, rh) + (dot(lh, rl) + dot(ll, rh))


def dot(left, right):
    return jnp.dot(left, right, preferred_element_type=jnp.float32)


def on_diagonal(order):
    rows = lax.broadcasted_iota(jnp.int32, (order, order), 0)
    return rows == lax.broadcasted_iota(jnp.int32, (order, order), 1)


def residual(matrix):
    order = matrix.shape[-1]
    same = on_diagonal(order)
    picked = jnp.where(same, matrix, 0.0)
    total = jnp.sum(jnp.sum(picked, axis=0, keepdims=True), axis=1, keepdims=True)
    scale = order / total
    return jnp.where(same, 1.0, 0.0) - matrix * scale, scale


def invert(matrix):
    rest, scale = residual(matrix)
    halves = split(rest)
    square = multiply(halves, halves)
    cube = multiply(halves, split(square))
    eye = jnp.where(on_diagonal(matrix.shape[-1]), 1.0, 0.0)
    return (eye + (rest + (square + cube))) * scale


def first_kernel(diag, low, up, rhs, scaled_up, scaled_low, scaled_rhs, diag_v, low_v, up_v, rhs_v, sems):
    pairs = ((diag, diag_v), (up, up_v), (low, low_v), (rhs, rhs_v))
    copies = [pltpu.make_async_copy(*pair, sems.at[place]) for place, pair in enumerate(pairs)]
    for copy in copies:
        copy.start()
    copies[0].wait()
    pivot = split(invert(diag_v[...]))
    copies[1].wait()
    scaled_up[...] = multiply(pivot, split(up_v[...]))
    copies[2].wait()
    scaled_low[...] = multiply(pivot, split(low_v[...]))
    copies[3].wait()
    scaled_rhs[...] = multiply(pivot, split(rhs_v[...]))


def vector_kernel(scaled_up, scaled_low, scaled_rhs, guess_l, guess_r, to_up, to_down):
    cols = scaled_rhs.shape[1]
    value = scaled_rhs[...]
    to_up[:, :cols] = value
    to_down[:, :cols] = value
    to_up[:, cols:] = multiply(split(scaled_low[...]), split(guess_l[...]))
    to_down[:, cols:] = multiply(split(scaled_up[...]), split(guess_r[...]))


def second_kernel(diag, low, up, up_l, low_r, diag1, pivot1, to_up, to_down):
    low_halves, up_halves = split(low[...]), split(up[...])
    value = diag[...] - multiply(low_halves, split(up_l[...])) - multiply(up_halves, split(low_r[...]))
    diag1[...] = value
    pivot = invert(value)
    pivot1[...] = pivot
    halves = split(pivot)
    to_up[...] = multiply(halves, up_halves)
    to_down[...] = multiply(halves, low_halves)


def middle_kernel(low, up, rhs, pivot1, vec_l, vec_r, rhs1, to_up, to_down):
    cols = rhs.shape[1]
    lv = multiply(split(low[...]), split(vec_l[...]))
    uv = multiply(split(up[...]), split(vec_r[...]))
    value = rhs[...] - lv[:, :cols] - uv[:, :cols]
    rhs1[...] = value
    pivot = split(pivot1[...])
    to_up[...] = multiply(pivot, split(value + lv[:, cols:]))
    to_down[...] = multiply(pivot, split(value + uv[:, cols:]))


def pair_kernel(left, right, out):
    out[...] = multiply(split(left[...]), split(right[...]))


def two_pairs_kernel(left_a, right_a, left_b, right_b, out_a, out_b):
    out_a[...] = multiply(split(left_a[...]), split(right_a[...]))
    out_b[...] = multiply(split(left_b[...]), split(right_b[...]))


def triple(first, second, third):
    return multiply(split(multiply(split(first), split(second))), split(third))


def before_last_kernel(base, first, second, third, out):
    out[...] = base[...] - triple(first[...], second[...], third[...])


def last_kernel(base, first, second, third, rest, scale):
    value, factor = residual(base[...] - triple(first[...], second[...], third[...]))
    rest[...] = value
    scale[...] = jnp.broadcast_to(factor, scale.shape)


def final_kernel(rest, scale, rhs1, low, up, d_l, d_r, out):
    inner = rhs1[...] + multiply(split(low[...]), split(d_l[...])) + multiply(split(up[...]), split(d_r[...]))
    halves = split(rest[...])
    part = inner + multiply(halves, split(multiply(halves, split(inner))))
    out[...] = (part + multiply(halves, split(part))) * scale[0:1, 0:1]


def call(kernel, outs, *args, weight=0, limit=VMEM_LIMIT, **options):
    in_vmem = pl.BlockSpec(memory_space=pltpu.VMEM)
    options = {"in_specs": [in_vmem] * len(args)} | options
    return pl.pallas_call(
        kernel,
        out_shape=[jax.ShapeDtypeStruct(shape, jnp.float32) for shape in outs],
        out_specs=[in_vmem] * len(outs),
        compiler_params=pltpu.CompilerParams(vmem_limit_bytes=limit),
        cost_estimate=pl.CostEstimate(flops=weight, bytes_accessed=0, transcendentals=0),
        **options,
    )(*args)


def body(diagonal, lower, upper, right_side, guess):
    diag, low, up, rhs = diagonal[0], lower[0], upper[0], right_side[0]
    square, tall = diag.shape, rhs.shape
    wide = (tall[0], 2 * tall[1])
    guess_l = shifted(guess[0], 1)
    guess_r = shifted(guess[0], -1)
    scaled_up, scaled_low, scaled_rhs = call(
        first_kernel,
        (square, square, tall),
        *(diag, low, up, rhs),
        limit=FIRST_LIMIT,
        in_specs=[pl.BlockSpec(memory_space=pl.ANY)] * 4,
        scratch_shapes=[pltpu.VMEM(shape, jnp.float32) for shape in (square, square, square, tall)]
        + [pltpu.SemaphoreType.DMA((4,))],
    )
    up_l = shifted(scaled_up, 1)
    low_r = shifted(scaled_low, -1)
    to_up, to_down = call(
        vector_kernel, (wide, wide), scaled_up, scaled_low, scaled_rhs, guess_l, guess_r, weight=VECTOR_WEIGHT
    )
    vec_l = shifted(to_up, 1)
    vec_r = shifted(to_down, -1)
    diag1, pivot1, next_up, next_down = call(second_kernel, (square,) * 4, diag, low, up, up_l, low_r)
    next_r = shifted(next_down, -1)
    next_l = shifted(next_up, 1)
    rhs1, w_up, w_down = call(
        middle_kernel, (tall,) * 3, low, up, rhs, pivot1, vec_l, vec_r, weight=MIDDLE_WEIGHT
    )
    w_l = shifted(w_up, 1)
    w_r = shifted(w_down, -1)
    scaled_low, scaled_up, _, _ = lax.optimization_barrier((scaled_low, scaled_up, w_up, w_down))
    (pass_up,) = call(pair_kernel, (square,), scaled_low, next_l)
    (pass_down,) = call(pair_kernel, (square,), scaled_up, next_r)
    pass_l = shifted(pass_up, 1)
    pass_r = shifted(pass_down, -1)
    w_l, w_r, _, _ = lax.optimization_barrier((w_l, w_r, pass_up, pass_down))
    d_up, d_down = call(two_pairs_kernel, (tall, tall), scaled_low, w_l, scaled_up, w_r, weight=PASS_WEIGHT)
    d_l = shifted(d_up, 1)
    d_r = shifted(d_down, -1)
    (part2,) = call(before_last_kernel, (square,), diag1, low, pass_l, up_l)
    rest, scale = call(last_kernel, (square, (8, 128)), part2, up, pass_r, low_r)
    d_l, d_r, rest = lax.optimization_barrier((d_l, d_r, rest))
    (out,) = call(final_kernel, (tall,), rest, scale, rhs1, low, up, d_l, d_r)
    return out[None]


def solution(mesh):
    spec = P(AXES, None, None)
    return jax.shard_map(
        body,
        mesh=mesh,
        in_specs=(spec,) * 5,
        out_specs=spec,
        check_vma=False,
    )
```

```python
import jax
import jax.numpy as jnp
from jax import lax
from jax.experimental import pallas as pl
from jax.experimental.pallas import tpu as pltpu
from jax.sharding import PartitionSpec as P

AXES = ("row", "col")

VECTOR_WEIGHT = 10**10
PASS_WEIGHT = 10**10
MIDDLE_WEIGHT = 10**10

VMEM_LIMIT = 24 * 1024 * 1024
FIRST_LIMIT = 60 * 1024 * 1024


def shifted(value, steps):
    count = lax.axis_size(AXES)
    initial, last = (max(0, -steps), min(count, count - steps))
    return lax.ppermute(value, AXES, [(source, source + steps) for source in range(initial, last)])


def split(value):
    high = value.astype(jnp.bfloat16)
    return high, (value - high.astype(jnp.float32)).astype(jnp.bfloat16)


def multiply(left, right):
    (lh, ll), (rh, rl) = left, right
    cols = rh.shape[1]
    if cols <= 128:
        both = dot(lh, jnp.concatenate([rh, rl], axis=1))
        return both[:, :cols] + (both[:, cols:] + dot(ll, rh))
    return dot(lh, rh) + (dot(lh, rl) + dot(ll, rh))


def dot(left, right):
    return jnp.dot(left, right, preferred_element_type=jnp.float32)


def on_diagonal(order):
    rows = lax.broadcasted_iota(jnp.int32, (order, order), 0)
    return rows == lax.broadcasted_iota(jnp.int32, (order, order), 1)


def residual(matrix):
    order = matrix.shape[-1]
    same = on_diagonal(order)
    picked = jnp.where(same, matrix, 0.0)
    total = jnp.sum(jnp.sum(picked, axis=0, keepdims=True), axis=1, keepdims=True)
    scale = order / total
    return jnp.where(same, 1.0, 0.0) - matrix * scale, scale


def invert(matrix):
    rest, scale = residual(matrix)
    halves = split(rest)
    square = multiply(halves, halves)
    cube = multiply(halves, split(square))
    eye = jnp.where(on_diagonal(matrix.shape[-1]), 1.0, 0.0)
    return (eye + (rest + (square + cube))) * scale


def first_kernel(diag, low, up, rhs, scaled_up, scaled_low, scaled_rhs, diag_v, low_v, up_v, rhs_v, sems):
    pairs = ((diag, diag_v), (up, up_v), (low, low_v), (rhs, rhs_v))
    copies = [pltpu.make_async_copy(*pair, sems.at[place]) for place, pair in enumerate(pairs)]
    for copy in copies:
        copy.start()
    copies[0].wait()
    pivot = split(invert(diag_v[...]))
    copies[1].wait()
    scaled_up[...] = multiply(pivot, split(up_v[...]))
    copies[2].wait()
    scaled_low[...] = multiply(pivot, split(low_v[...]))
    copies[3].wait()
    scaled_rhs[...] = multiply(pivot, split(rhs_v[...]))


def vector_kernel(scaled_up, scaled_low, scaled_rhs, guess_l, guess_r, to_up, to_down):
    cols = scaled_rhs.shape[1]
    value = scaled_rhs[...]
    to_up[:, :cols] = value
    to_down[:, :cols] = value
    to_up[:, cols:] = multiply(split(scaled_low[...]), split(guess_l[...]))
    to_down[:, cols:] = multiply(split(scaled_up[...]), split(guess_r[...]))


def second_kernel(diag, low, up, up_l, low_r, diag1, pivot1, to_up, to_down):
    low_halves, up_halves = split(low[...]), split(up[...])
    value = diag[...] - multiply(low_halves, split(up_l[...])) - multiply(up_halves, split(low_r[...]))
    diag1[...] = value
    pivot = invert(value)
    pivot1[...] = pivot
    halves = split(pivot)
    to_up[...] = multiply(halves, up_halves)
    to_down[...] = multiply(halves, low_halves)


def middle_kernel(low, up, rhs, pivot1, vec_l, vec_r, rhs1, to_up, to_down):
    cols = rhs.shape[1]
    lv = multiply(split(low[...]), split(vec_l[...]))
    uv = multiply(split(up[...]), split(vec_r[...]))
    value = rhs[...] - lv[:, :cols] - uv[:, :cols]
    rhs1[...] = value
    pivot = split(pivot1[...])
    to_up[...] = multiply(pivot, split(value + lv[:, cols:]))
    to_down[...] = multiply(pivot, split(value + uv[:, cols:]))


def pair_kernel(left, right, out):
    out[...] = multiply(split(left[...]), split(right[...]))


def two_pairs_kernel(left_a, right_a, left_b, right_b, out_a, out_b):
    out_a[...] = multiply(split(left_a[...]), split(right_a[...]))
    out_b[...] = multiply(split(left_b[...]), split(right_b[...]))


def triple(first, second, third):
    return multiply(split(multiply(split(first), split(second))), split(third))


def before_last_kernel(base, first, second, third, out):
    out[...] = base[...] - triple(first[...], second[...], third[...])


def last_kernel(base, first, second, third, rest, scale):
    value, factor = residual(base[...] - triple(first[...], second[...], third[...]))
    rest[...] = value
    scale[...] = jnp.broadcast_to(factor, scale.shape)


def final_kernel(rest, scale, rhs1, low, up, d_l, d_r, out):
    inner = rhs1[...] + multiply(split(low[...]), split(d_l[...])) + multiply(split(up[...]), split(d_r[...]))
    halves = split(rest[...])
    part = inner + multiply(halves, split(multiply(halves, split(inner))))
    out[...] = (part + multiply(halves, split(part))) * scale[0:1, 0:1]


def call(kernel, outs, *args, weight=0, limit=VMEM_LIMIT, **options):
    in_vmem = pl.BlockSpec(memory_space=pltpu.VMEM)
    options = {"in_specs": [in_vmem] * len(args)} | options
    return pl.pallas_call(
        kernel,
        out_shape=[jax.ShapeDtypeStruct(shape, jnp.float32) for shape in outs],
        out_specs=[in_vmem] * len(outs),
        compiler_params=pltpu.CompilerParams(vmem_limit_bytes=limit),
        cost_estimate=pl.CostEstimate(flops=weight, bytes_accessed=0, transcendentals=0),
        **options,
    )(*args)


def body(diagonal, lower, upper, right_side, guess):
    diag, low, up, rhs = diagonal[0], lower[0], upper[0], right_side[0]
    square, tall = diag.shape, rhs.shape
    wide = (tall[0], 2 * tall[1])
    guess_l = shifted(guess[0], 1)
    guess_r = shifted(guess[0], -1)
    scaled_up, scaled_low, scaled_rhs = call(
        first_kernel,
        (square, square, tall),
        *(diag, low, up, rhs),
        limit=FIRST_LIMIT,
        in_specs=[pl.BlockSpec(memory_space=pl.ANY)] * 4,
        scratch_shapes=[pltpu.VMEM(shape, jnp.float32) for shape in (square, square, square, tall)]
        + [pltpu.SemaphoreType.DMA((4,))],
    )
    up_l = shifted(scaled_up, 1)
    low_r = shifted(scaled_low, -1)
    to_up, to_down = call(
        vector_kernel, (wide, wide), scaled_up, scaled_low, scaled_rhs, guess_l, guess_r, weight=VECTOR_WEIGHT
    )
    low_r, to_up, to_down = lax.optimization_barrier((low_r, to_up, to_down))
    vec_l = shifted(to_up, 1)
    vec_r = shifted(to_down, -1)
    diag1, pivot1, next_up, next_down = call(second_kernel, (square,) * 4, diag, low, up, up_l, low_r)
    next_r = shifted(next_down, -1)
    next_l = shifted(next_up, 1)
    rhs1, w_up, w_down = call(
        middle_kernel, (tall,) * 3, low, up, rhs, pivot1, vec_l, vec_r, weight=MIDDLE_WEIGHT
    )
    w_l = shifted(w_up, 1)
    w_r = shifted(w_down, -1)
    scaled_low, scaled_up, _, _ = lax.optimization_barrier((scaled_low, scaled_up, w_up, w_down))
    (pass_up,) = call(pair_kernel, (square,), scaled_low, next_l)
    (pass_down,) = call(pair_kernel, (square,), scaled_up, next_r)
    pass_l = shifted(pass_up, 1)
    pass_r = shifted(pass_down, -1)
    w_l, w_r, _, _ = lax.optimization_barrier((w_l, w_r, pass_up, pass_down))
    d_up, d_down = call(two_pairs_kernel, (tall, tall), scaled_low, w_l, scaled_up, w_r, weight=PASS_WEIGHT)
    d_l = shifted(d_up, 1)
    d_r = shifted(d_down, -1)
    (part2,) = call(before_last_kernel, (square,), diag1, low, pass_l, up_l)
    rest, scale = call(last_kernel, (square, (8, 128)), part2, up, pass_r, low_r)
    d_l, d_r, rest = lax.optimization_barrier((d_l, d_r, rest))
    (out,) = call(final_kernel, (tall,), rest, scale, rhs1, low, up, d_l, d_r)
    return out[None]


def solution(mesh):
    spec = P(AXES, None, None)
    return jax.shard_map(
        body,
        mesh=mesh,
        in_specs=(spec,) * 5,
        out_specs=spec,
        check_vma=False,
    )
```
